256 devices in a mesh: grp: 8 (over z), seq: 32 (over y, x, core).
Axes of the slice: x: 4, y: 4, z: 8, core: 2. Of those that a mesh axis runs over, the one named last changes fastest.
Arguments:
- queries: bfloat16 [64, 4, 64, 576], P('grp'), parts along dimension 0, may hold values from -190 to 190
- latent_cache: bfloat16 [64, 32768, 576], P('grp', 'seq'), parts along dimension 0, may hold values from -4 to 4
- context_lengths: int32 [64], P('grp'), parts along dimension 0, may hold values from 8192 to 32768, as said below
- value_up: bfloat16 [64, 512, 128], P('seq'), may hold values from -0.5 to 0.5
- output_projection_rows: bfloat16 [8192, 7168], P('seq'), may hold values from -0.25 to 0.25
Outputs:
- attention_out: bfloat16 [64, 4, 7168], P('grp', None, 'seq'), parts along dimension 0
The draws below stay inside these ranges and needn't reach their ends.
There are 8 independent parts, one for each index of `grp`. The reference program is written for one: setup_inputs(seed, part) draws one part's arguments, and reference() takes and returns one part's arrays. A program takes and returns all parts, laid end to end along the dimension named above; an argument that names none is the same for every part. Nothing has to cross between parts.
Inputs may be any that keep to these rules, and one draw needn't show every extreme that they name: `context_lengths`: in every draw one request holds exactly 32768 tokens.
All inputs are finite; a program needn't handle non-finite values.
Results may differ from the reference program's by a relative error of at most 0.0058.
Values sent between devices are 32-bit elements; how exact they have to be, the bound alone decides.
A program may use at most 128 MiB of HBM per device.

```python
import jax
import jax.numpy as jnp
from jax import lax

B = 8
NQ = 4
CTX_DEV = 1024
H = 64
KVR = 512
VD = 128
D = 7168
LAT = 576
CTX = 32768
N_SEQ = 32


def draw_queries(key, part):
    own_key = jax.random.fold_in(key, 7)
    queries = 1.5 * jnp.clip(jax.random.normal(own_key, (B, NQ, H, LAT), jnp.float32), -4.0, 4.0)
    return queries.astype(jnp.bfloat16)


def draw_latent_cache(key, part):
    own_key = jax.random.fold_in(key, 5)
    latent = jnp.clip(jax.random.normal(own_key, (B, CTX, LAT), jnp.float32), -4.0, 4.0)
    return latent.astype(jnp.bfloat16)


def draw_context_lengths(key, part):
    own_key = jax.random.fold_in(key, 3)
    key_draw, key_order = jax.random.split(own_key, 2)
    lengths = jax.random.randint(key_draw, (B,), CTX // 4, CTX + 1)
    longest = jax.random.randint(key_order, (), 0, B)
    lengths = lengths.at[longest].set(CTX)
    return lengths.astype(jnp.int32)


def level_of(key, shape, shards, smallest, high):
    factor_of, own = 1.0, jax.random.fold_in(key, 6)
    for axis_at, shards_of in shards:
        heights = jnp.exp(jax.random.uniform(jax.random.fold_in(own, axis_at), (shards_of,), jnp.float32, smallest / len(shards), high / len(shards)))
        factor_of = factor_of * jnp.repeat(heights, shape[axis_at] // shards_of).reshape([-1 if axis == axis_at else 1 for axis in range(len(shape))])
    return factor_of


def gaussian(rng, shape, scale, limit, shards=(), held_as=jnp.bfloat16):
    array = scale * jax.random.normal(rng, shape, jnp.float32)
    if shards:
        array = array * level_of(rng, shape, shards, -0.22, 0.18)
    return jnp.clip(array, -limit, limit).astype(held_as)


def setup_inputs(seed: int = 0, part: int = 0) -> dict:
    streams_of = jax.random.split(jax.random.key(seed), 6)
    own_keys = jax.random.split(jax.random.fold_in(streams_of[5], part), 6)
    queries = draw_queries(jax.random.fold_in(jax.random.fold_in(streams_of[5], part), 71), part)
    latent_cache = draw_latent_cache(jax.random.fold_in(jax.random.fold_in(streams_of[5], part), 71), part)
    context_lengths = draw_context_lengths(jax.random.fold_in(jax.random.fold_in(streams_of[5], part), 71), part)
    value_up = gaussian(streams_of[3], (H, KVR, VD), (KVR // 4) ** -0.5, 0.5, ((0, 32),))
    output_projection_rows = gaussian(streams_of[4], (H * VD, D), (H * VD // 16) ** -0.5, 0.25, ((0, 32),))
    return dict(queries=queries, latent_cache=latent_cache, context_lengths=context_lengths, value_up=value_up, output_projection_rows=output_projection_rows)


score_scale = 0.07216878364870323
empty_mark = -1.0e30


def local_partial(queries, cache_rows, context_lengths, first_token):
    query_count = queries.shape[1]
    shard_width = cache_rows.shape[1]
    scores = jnp.einsum("bqhc,btc->bqht", queries.astype(jnp.float32), cache_rows.astype(jnp.float32)) * score_scale
    position = first_token + jnp.arange(shard_width, dtype=jnp.int32)
    row_limit = context_lengths[:, None] - (query_count - 1) + jnp.arange(query_count, dtype=jnp.int32)[None, :]
    visible = position[None, None, None, :] < row_limit[:, :, None, None]
    masked = jnp.where(visible, scores, empty_mark)
    row_peak = jnp.max(masked, axis=3)
    weights = jnp.where(visible, jnp.exp(masked - row_peak[..., None]), 0.0)
    row_rescale = jnp.maximum(jnp.sum(weights, axis=3), 1.0)
    weights_low = lax.optimization_barrier(weights.astype(jnp.bfloat16)).astype(jnp.float32)
    values = jnp.einsum("bqht,btc->bqhc", weights_low, cache_rows[:, :, :KVR].astype(jnp.float32))
    return values / row_rescale[..., None], row_peak + jnp.log(row_rescale)


def reference(queries, latent_cache, context_lengths, value_up, output_projection_rows):
    def device_partial_terms(shard_index):
        first_token = shard_index * CTX_DEV
        cache_rows = lax.dynamic_slice_in_dim(latent_cache, first_token, CTX_DEV, 1)
        return local_partial(queries, cache_rows, context_lengths, first_token)

    partials, log_sums = lax.map(device_partial_terms, jnp.arange(N_SEQ, dtype=jnp.int32))
    greatest_score = jnp.max(log_sums, axis=0)
    shares = jnp.exp(log_sums - greatest_score[None])
    attended = jnp.sum(shares[..., None] * partials, axis=0) / jnp.sum(shares, axis=0)[..., None]
    attended_low = lax.optimization_barrier(attended.astype(jnp.bfloat16)).astype(jnp.float32)
    head_out = jnp.einsum("bqhc,hcv->bqhv", attended_low, value_up.astype(jnp.float32))
    head_low = lax.optimization_barrier(head_out.astype(jnp.bfloat16)).astype(jnp.float32)
    flattened_heads = head_low.reshape(head_low.shape[0], head_low.shape[1], -1)
    final_output = jnp.einsum("msp,pc->msc", flattened_heads, output_projection_rows.astype(jnp.float32))
    return final_output.astype(jnp.bfloat16)
```

```python
import functools

import jax
import jax.numpy as jnp
from jax import lax
from jax.experimental import pallas as pl
from jax.experimental.pallas import tpu as pltpu
from jax.sharding import PartitionSpec as P

MESH = pl.DeviceIdType.MESH
f32, bf16 = jnp.float32, jnp.bfloat16

B, NQ, H, T, C, L, V, D = 8, 4, 64, 1024, 576, 512, 128, 7168
ROWS = NQ * H
DEV_COLS = D // 32
C2 = 0.07216878364870323 * 1.4426950408889634
EMPTY = -1e30
TICK_D, TICK_E = 4, 7


def iota(shape, dim):
    return lax.broadcasted_iota(jnp.int32, shape, dim)


def column(tile, lane):
    return jnp.broadcast_to(tile[:, lane : lane + 1], (8, 128))


def kernel(
    q_hbm, k_hbm, ctx_ref, vu_hbm, w_hbm, o_ref,
    q, k, vu, w, perm,
    cs, cr, p1, p1r, p2, p2r, att, ys, yr, z1r, z2, z2r,
    lsem, cs_s, cs_r, p1_s, p1_r, p2_s, p2_r, y_s, y_r, z1_s, z1_r, z2_s, z2_r,
):
    me = lax.axis_index("seq")
    c, x, y = me % 2, (me // 2) % 4, me // 8

    def device(yy, xx, cc):
        return (yy * 4 + xx) * 2 + cc

    other = device(y, x, 1 - c)

    def along(par, r):
        return device((y + r * par) % 4, (x + r * (1 - par)) % 4, c)

    barrier = pltpu.get_barrier_semaphore()
    partners = [other] + [along(par, r) for par in (0, 1) for r in (1, 2, 3)]
    for to in partners:
        pl.semaphore_signal(barrier, inc=1, device_id={"seq": to}, device_id_type=MESH)

    def load_q(b):
        return pltpu.make_async_copy(q_hbm.at[b], q.at[b], lsem.at[0, b])

    def load_k(b):
        return pltpu.make_async_copy(k_hbm.at[b], k.at[b], lsem.at[1, b])

    load_vu = pltpu.make_async_copy(vu_hbm, vu, lsem.at[2, 0])
    load_w = pltpu.make_async_copy(w_hbm, w, lsem.at[2, 1])
    for b in range(B):
        load_q(b).start()
        load_k(b).start()
    load_vu.start()
    load_w.start()

    row, col = iota((ROWS, ROWS), 0), iota((ROWS, ROWS), 1)
    r2, r1, cc = (row >> 3) & 3, (row >> 5) & 3, (row >> 7) & 1
    for par in (0, 1):
        rx, ry = (r1, r2) if par == 0 else (r2, r1)
        chip = ((y + ry) & 3) * 4 + ((x + rx) & 3)
        head = (chip * 2 + ((c + cc) & 1)) * 2 + ((row >> 2) & 1)
        perm[par] = jnp.where(col == (row & 3) * H + head, 1.0, 0.0).astype(bf16)

    pl.semaphore_wait(barrier, len(partners))

    lane = iota((8, 128), 1)

    def remote(src, dst, ssem, rsem, to):
        return pltpu.make_async_remote_copy(
            src_ref=src, dst_ref=dst, send_sem=ssem, recv_sem=rsem,
            device_id={"seq": to}, device_id_type=MESH,
        )

    def copy_c(b):
        return remote(cs.at[b], cr.at[b], cs_s.at[b], cs_r.at[b], other)

    def copy_p1(b, r):
        return remote(
            p1.at[b, r], p1r.at[b, r - 1], p1_s.at[b, r - 1], p1_r.at[b, r - 1], along(b % 2, r)
        )

    def copy_p2(b, r):
        return remote(
            p2.at[b, r], p2r.at[b, r - 1], p2_s.at[b, r - 1], p2_r.at[b, r - 1], along(1 - b % 2, r)
        )

    def attend(b):
        load_q(b).wait()
        load_k(b).wait()
        queries = jnp.dot(perm[b % 2], q[b], preferred_element_type=f32).astype(bf16)
        s = jnp.dot(queries, k[b], preferred_element_type=f32)
        limit = (ctx_ref[b] - (NQ - 1) - me * T) + (iota((ROWS, 1), 0) & 3)
        s = jnp.where(iota((ROWS, T), 1) < limit, s, EMPTY)
        peak = jnp.max(s, axis=1, keepdims=True)
        e = jnp.exp2((s - peak) * C2)
        total = jnp.sum(e, axis=1, keepdims=True)
        acc = lax.dot_general(
            e.astype(bf16), k[b, :L, :], (((1,), (1,)), ((), ())), preferred_element_type=f32
        )
        peak = peak * C2
        for half, ref in ((0, p1), (1, cs)):
            for g in range(4):
                stat = jnp.zeros((8, 128), f32)
                for t in range(4):
                    at = ((half * 4 + g) * 4 + t) * 8
                    stat = jnp.where(lane == t, peak[at : at + 8], stat)
                    stat = jnp.where(lane == 64 + t, total[at : at + 8], stat)
                    for i in range(4):
                        ref[b, g, t * 4 + i] = acc[at : at + 8, i * 128 : i * 128 + 128]
                ref[b, g, 16] = stat
        copy_c(b).start()

    def merge_stats(stats):
        top = functools.reduce(jnp.maximum, stats)
        shares = [jnp.exp2(s - top) for s in stats]
        total = sum(pltpu.roll(f, 64, 1) * s for f, s in zip(shares, stats))
        return shares, jnp.where(lane < 64, top, total)

    def merge_core(b):
        copy_c(b).wait_recv()
        for g in range(4):
            shares, stat = merge_stats([p1[b, g, 16], cr[b, g, 16]])
            for t in range(4):
                f0, f1 = column(shares[0], t), column(shares[1], t)
                for i in range(4):
                    at = t * 4 + i
                    p1[b, g, at] = f0 * p1[b, g, at] + f1 * cr[b, g, at]
            p1[b, g, 16] = stat
        for r in (1, 2, 3):
            copy_p1(b, r).start()

    def merge_first(b):
        for r in (1, 2, 3):
            copy_p1(b, r).wait_recv()
        parts = [p1.at[b, 0]] + [p1r.at[b, r] for r in range(3)]
        shares, stat = merge_stats([part[16] for part in parts])
        for t in range(4):
            f = [column(s, t) for s in shares]
            for i in range(4):
                p2[b, t, i] = sum(f[n] * parts[n][t * 4 + i] for n in range(4))
            p2[b, t, 4] = stat
        for r in (1, 2, 3):
            copy_p2(b, r).start()

    def merge_second(b):
        for r in (1, 2, 3):
            copy_p2(b, r).wait_recv()
        parts = [p2.at[b, 0]] + [p2r.at[b, r] for r in range(3)]
        peaks = [column(part[4], t) for t, part in enumerate(parts)]
        totals = [column(part[4], 64 + t) for t, part in enumerate(parts)]
        top = functools.reduce(jnp.maximum, peaks)
        f = [jnp.exp2(p - top) for p in peaks]
        inverse = 1.0 / sum(a * b for a, b in zip(f, totals))
        for i in range(4):
            att[b, :, i * 128 : i * 128 + 128] = sum(f[n] * parts[n][i] for n in range(4)) * inverse

    def tick(i, _):
        @pl.when(i < B)
        def _():
            attend(i)

        @pl.when((i >= 1) & (i < B + 1))
        def _():
            merge_core(i - 1)

        @pl.when((i >= TICK_D) & (i < B + TICK_D))
        def _():
            merge_first(i - TICK_D)

        @pl.when((i >= TICK_E) & (i < B + TICK_E))
        def _():
            merge_second(i - TICK_E)

        return 0

    lax.fori_loop(0, B + TICK_E, tick, 0)

    load_vu.wait()
    load_w.wait()
    low = att[...].reshape(B * 8, L).astype(bf16)
    up = [jnp.dot(low, vu[n], preferred_element_type=f32) for n in range(2)]
    sub = iota((8, 128), 0)
    rows = []
    for b in range(0, B, 2):
        a = [up[n][8 * b : 8 * b + 8] for n in range(2)]
        z = [up[n][8 * b + 8 : 8 * b + 16] for n in range(2)]
        h0 = jnp.where(sub < 4, a[0], pltpu.roll(z[0], 4, 0))
        h1 = jnp.where(sub < 4, pltpu.roll(a[1], 4, 0), z[1])
        rows.append(jnp.concatenate([h0, h1], axis=1))
    head_out = jnp.concatenate(rows, axis=0).astype(bf16)

    def copy_y(part):
        return remote(ys.at[1 - c, part], yr.at[part], y_s.at[part], y_r.at[part], other)

    mine = (x, y)

    def copy_z1(part, r):
        return remote(
            ys.at[c, part, (mine[part] + r) % 4], z1r.at[part, r - 1],
            z1_s.at[part, r - 1], z1_r.at[part, r - 1], along(part, r),
        )

    def copy_z2(part, r):
        return remote(
            z2.at[part, (mine[1 - part] + r) % 4], z2r.at[part, r - 1],
            z2_s.at[part, r - 1], z2_r.at[part, r - 1], along(1 - part, r),
        )

    for four in range(8):
        out = jnp.dot(head_out, w[:, four * 896 : four * 896 + 896], preferred_element_type=f32)
        for dev in range(4):
            start = dev * DEV_COLS
            low_tile = start // 128 * 128
            wide = out[:, low_tile : min(low_tile + 384, 896)]
            width = wide.shape[1]
            if start != low_tile:
                wide = pltpu.roll(wide, width - (start - low_tile), 1)
            chip = four * 2 + dev // 2
            yy, xx = chip // 4, chip % 4
            for part in range(2):
                first, second = (xx, yy) if part == 0 else (yy, xx)
                for rt in range(2):
                    for i in range(2):
                        ys[dev % 2, part, first, second, rt * 2 + i] = wide[
                            part * 16 + rt * 8 : part * 16 + rt * 8 + 8, i * 128 : i * 128 + 128
                        ]
    for part in range(2):
        copy_y(part).start()
    for part in range(2):
        copy_y(part).wait_recv()
        for first in range(4):
            ys[c, part, first] = ys[c, part, first] + yr[part, first]
        for r in (1, 2, 3):
            copy_z1(part, r).start()
    for part in range(2):
        for r in (1, 2, 3):
            copy_z1(part, r).wait_recv()
        z2[part] = ys[c, part, mine[part]] + z1r[part, 0] + z1r[part, 1] + z1r[part, 2]
        for r in (1, 2, 3):
            copy_z2(part, r).start()
    for part in range(2):
        for r in (1, 2, 3):
            copy_z2(part, r).wait_recv()
        done = z2[part, mine[1 - part]] + z2r[part, 0] + z2r[part, 1] + z2r[part, 2]
        for rt in range(2):
            tile = jnp.concatenate([done[rt * 2], done[rt * 2 + 1]], axis=1)[:, :DEV_COLS]
            at = part * 16 + rt * 8
            o_ref[at : at + 8, :] = tile

    def drain(b, _):
        copy_c(b).wait_send()
        for r in (1, 2, 3):
            copy_p1(b, r).wait_send()
            copy_p2(b, r).wait_send()
        return 0

    lax.fori_loop(0, B, drain, 0)
    for part in range(2):
        copy_y(part).wait_send()
        for r in (1, 2, 3):
            copy_z1(part, r).wait_send()
            copy_z2(part, r).wait_send()


def local(queries, latent_cache, context_lengths, value_up, output_projection_rows):
    tile = (8, 128)
    dma = pltpu.SemaphoreType.DMA
    out = pl.pallas_call(
        kernel,
        out_shape=jax.ShapeDtypeStruct((B * NQ, DEV_COLS), f32),
        in_specs=[
            pl.BlockSpec(memory_space=pl.ANY),
            pl.BlockSpec(memory_space=pl.ANY),
            pl.BlockSpec(memory_space=pltpu.SMEM),
            pl.BlockSpec(memory_space=pl.ANY),
            pl.BlockSpec(memory_space=pl.ANY),
        ],
        out_specs=pl.BlockSpec(memory_space=pltpu.VMEM),
        scratch_shapes=[
            pltpu.VMEM((B, ROWS, C), bf16),
            pltpu.VMEM((B, C, T), bf16),
            pltpu.VMEM((2, L, V), bf16),
            pltpu.VMEM((2 * V, D), bf16),
            pltpu.VMEM((2, ROWS, ROWS), bf16),
            pltpu.VMEM((B, 4, 17) + tile, f32),
            pltpu.VMEM((B, 4, 17) + tile, f32),
            pltpu.VMEM((B, 4, 17) + tile, f32),
            pltpu.VMEM((B, 3, 17) + tile, f32),
            pltpu.VMEM((B, 4, 5) + tile, f32),
            pltpu.VMEM((B, 3, 5) + tile, f32),
            pltpu.VMEM((B, 8, L), f32),
            pltpu.VMEM((2, 2, 4, 4, 4) + tile, f32),
            pltpu.VMEM((2, 4, 4, 4) + tile, f32),
            pltpu.VMEM((2, 3, 4, 4) + tile, f32),
            pltpu.VMEM((2, 4, 4) + tile, f32),
            pltpu.VMEM((2, 3, 4) + tile, f32),
            dma((3, B)),
            dma((B,)), dma((B,)),
            dma((B, 3)), dma((B, 3)),
            dma((B, 3)), dma((B, 3)),
            dma((2,)), dma((2,)),
            dma((2, 3)), dma((2, 3)),
            dma((2, 3)), dma((2, 3)),
        ],
        compiler_params=pltpu.CompilerParams(
            collective_id=0, has_side_effects=True, vmem_limit_bytes=56 * 2**20
        ),
        name="attend_and_project",
    )(
        queries.reshape(B, ROWS, C),
        jnp.swapaxes(latent_cache, 1, 2),
        context_lengths,
        value_up,
        output_projection_rows,
    )
    return out.reshape(B, NQ, DEV_COLS).astype(bf16)


def solution(mesh):
    placed = (
        P("grp", None, None, None),
        P("grp", "seq", None),
        P("grp"),
        P("seq", None, None),
        P("seq", None),
    )
    return jax.shard_map(
        local, mesh=mesh, in_specs=placed, out_specs=P("grp", None, "seq"), check_vma=False
    )
```

```python
import functools

import jax
import jax.numpy as jnp
from jax import lax
from jax.experimental import pallas as pl
from jax.experimental.pallas import tpu as pltpu
from jax.sharding import PartitionSpec as P

MESH = pl.DeviceIdType.MESH
f32, bf16 = jnp.float32, jnp.bfloat16

B, NQ, H, T, C, L, V, D = 8, 4, 64, 1024, 576, 512, 128, 7168
ROWS = NQ * H
DEV_COLS = D // 32
C2 = 0.07216878364870323 * 1.4426950408889634
EMPTY = -1e30
TICK_R, TICK_D = 3, 6
RELAYED = 6
GROUPS = ((0, 4), (4, 8))
CHIPS = sorted(
    [(dx, dy) for dy in range(4) for dx in range(4) if dx or dy],
    key=lambda o: -(min(o[0], 4 - o[0]) + min(o[1], 4 - o[1])),
)


def iota(shape, dim):
    return lax.broadcasted_iota(jnp.int32, shape, dim)


def column(tile, lane):
    return jnp.broadcast_to(tile[:, lane : lane + 1], (8, 128))


def blocks_transposed(tiles):
    sub = iota((8, 128), 0)
    low, even = sub < 4, (sub & 2) == 0
    half = [pltpu.roll(t, 4, 0) for t in tiles]
    a0, a2 = jnp.where(low, tiles[0], half[2]), jnp.where(low, half[0], tiles[2])
    a1, a3 = jnp.where(low, tiles[1], half[3]), jnp.where(low, half[1], tiles[3])
    out = []
    for p, r in ((a0, a1), (a2, a3)):
        out.append(jnp.where(even, p, pltpu.roll(r, 2, 0)))
        out.append(jnp.where(even, pltpu.roll(p, 6, 0), r))
    return out


def tile_at(second, part):
    return second * 4 + part + second // 2


def head_major(tile):
    sub = iota((8, 128), 0)
    out = tile
    for to, at in ((1, 2), (2, 4), (3, 6), (4, 1), (5, 3), (6, 5)):
        out = jnp.where(sub == to, pltpu.roll(tile, (to - at) % 8, 0), out)
    return out


def kernel(
    q_hbm, k_hbm, ctx_ref, vu_hbm, w_hbm, o_ref,
    q, k, vu, w, sc, pk,
    pc, cr, mg, rr, p1r, p2, p2r, att,
    lsem, cs_s, cs_r, r_s, r_r, p1_s, p1_r, p2_s, p2_r, y_s, y_r, z_s, z_r, *terms
):
    me = lax.axis_index("seq")
    c, x, y = me % 2, (me // 2) % 4, me // 8

    def device(yy, xx, cc):
        return (yy * 4 + xx) * 2 + cc

    other = device(y, x, 1 - c)

    def along(par, r):
        return device((y + r * par) % 4, (x + r * (1 - par)) % 4, c)

    def position(par):
        return x + (y - x) * par

    barrier = pltpu.get_barrier_semaphore()
    def chip_at(offset):
        return ((y + offset[1]) % 4) * 4 + (x + offset[0]) % 4

    partners = [other] + [along(par, r) for par in (0, 1) for r in (1, 2, 3)]
    for to in partners:
        pl.semaphore_signal(barrier, inc=1, device_id={"seq": to}, device_id_type=MESH)

    def load_q(b):
        return pltpu.make_async_copy(q_hbm.at[b], q.at[b], lsem.at[0, b])

    def load_k(b):
        return pltpu.make_async_copy(k_hbm.at[b], k.at[b], lsem.at[1, b])

    load_vu = pltpu.make_async_copy(vu_hbm, vu, lsem.at[2, 0])
    load_w = pltpu.make_async_copy(w_hbm, w, lsem.at[2, 1])
    for b in range(B):
        load_q(b).start()
        load_k(b).start()
    load_vu.start()
    load_w.start()

    lane = iota((8, 128), 1)

    def remote(src, dst, ssem, rsem, to):
        return pltpu.make_async_remote_copy(
            src_ref=src, dst_ref=dst, send_sem=ssem, recv_sem=rsem,
            device_id={"seq": to}, device_id_type=MESH,
        )

    def copy_c(b):
        return remote(pc.at[b, 1 - c], cr.at[b], cs_s.at[b], cs_r.at[b], other)

    def copy_p1(b, r):
        return remote(
            mg.at[b, (position(b % 2) + r) % 4], p1r.at[b, r - 1],
            p1_s.at[b, r - 1], p1_r.at[b, r - 1], along(b % 2, r),
        )

    def copy_p2(b, r):
        return remote(
            p2.at[b, (position(1 - b % 2) + r) % 4], p2r.at[b, r - 1],
            p2_s.at[b, r - 1], p2_r.at[b, r - 1], along(1 - b % 2, r),
        )

    def scores(b, slot):
        load_q(b).wait()
        load_k(b).wait()
        s = jnp.dot(q[b], k[b], preferred_element_type=f32)
        limit = (ctx_ref[b] - (NQ - 1) - me * T) + (iota((ROWS, 1), 0) >> 6)
        s = jnp.where(iota((ROWS, T), 1) < limit, s, EMPTY)
        sc[slot] = s
        pk[slot] = jnp.broadcast_to(jnp.max(s, axis=1, keepdims=True), (ROWS, 128))

    def attend(b, slot, following=True):
        if following:
            scores(b + 1, 1 - slot)
        peak = pk[slot]
        e = jnp.exp2((sc[slot] - peak[:, :1]) * C2)
        total = jnp.sum(e, axis=1, keepdims=True)
        acc = lax.dot_general(
            e.astype(bf16), k[b, :L, :], (((1,), (1,)), ((), ())), preferred_element_type=f32
        )
        both = jnp.where(iota((ROWS, 128), 1) < 64, peak * C2, total)
        stats = {}
        for eight in range(8):
            rows = [slice(n * 64 + eight * 8, n * 64 + eight * 8 + 8) for n in range(4)]
            for part in range(5):
                src = both if part == 4 else acc[:, part * 128 : part * 128 + 128]
                for n, tile in enumerate(blocks_transposed([src[r] for r in rows])):
                    chip, core = (eight * 4 + n) // 2, n % 2
                    yy, xx = chip // 4, chip % 4
                    first, second = (xx, yy) if slot == 0 else (yy, xx)
                    if part < 4:
                        pc[b, core, first, tile_at(second, part)] = tile
                    else:
                        before = stats.get((core, first), jnp.zeros((8, 128), f32))
                        stats[core, first] = jnp.where((lane & 63) == second, tile, before)
        for (core, first), tile in stats.items():
            pc[b, core, first, 8] = tile

    def merge_stats(stats):
        top = functools.reduce(jnp.maximum, stats)
        shares = [jnp.exp2(s - top) for s in stats]
        total = sum(pltpu.roll(f, 64, 1) * s for f, s in zip(shares, stats))
        return shares, jnp.where(lane < 64, top, total)

    def merge_core(b):
        copy_c(b).wait_recv()
        merged = [merge_stats([pc[b, c, g, 8], cr[b, g, 8]]) for g in range(4)]
        for g in range(4):
            shares, stat = merged[g]
            for t in range(4):
                f0, f1 = column(shares[0], t), column(shares[1], t)
                for i in range(4):
                    at = tile_at(t, i)
                    mg[b, g, at] = f0 * pc[b, c, g, at] + f1 * cr[b, g, at]
            mg[b, g, 8] = stat

    def copy_r(b, way):
        par = b % 2
        return remote(
            mg.at[b, (position(par) + 2) % 4, pl.ds(8 * way, 9)], rr.at[b, way],
            r_s.at[b, way], r_r.at[b, way], along(par, 1 + 2 * way),
        )

    def start_relay(b):
        for way in range(2):
            copy_r(b, way).start()

    def relay(b):
        for way in range(2):
            copy_r(b, way).wait_recv()
        for way in range(2):
            g = (position(b % 2) + 1 + 2 * way) % 4
            mine = mg[b, g, 8]
            shares, stat = merge_stats([mine, rr[b, way, 8 - 8 * way]])
            for t in (2 * way, 2 * way + 1):
                f0, f1 = column(shares[0], t), column(shares[1], t)
                for i in range(4):
                    at = tile_at(t, i)
                    mg[b, g, at] = f0 * mg[b, g, at] + f1 * rr[b, way, at - 8 * way]
            mg[b, g, 8] = jnp.where((lane & 63) // 2 == way, stat, mine)
            copy_p1(b, 1 + 2 * way).start()

    def send_p1(b):
        for r in (2, 1, 3):
            copy_p1(b, r).start()

    def merge_first(b, relayed):
        steps = (1, 3) if relayed else (1, 2, 3)
        for r in steps:
            copy_p1(b, r).wait_recv()
        parts = [mg.at[b, position(b % 2)]] + [p1r.at[b, r - 1] for r in steps]
        shares, stat = merge_stats([part[8] for part in parts])
        for t in range(4):
            f = [column(s, t) for s in shares]
            for i in range(4):
                p2[b, t, i] = sum(f[n] * parts[n][tile_at(t, i)] for n in range(len(parts)))
            p2[b, t, 4] = pltpu.roll(stat, 128 - t, 1) if t else stat
        for r in (2, 1, 3):
            copy_p2(b, r).start()

    def merge_second(b):
        for r in (1, 2, 3):
            copy_p2(b, r).wait_recv()
        parts = [p2.at[b, position(1 - b % 2)]] + [p2r.at[b, r] for r in range(3)]
        peaks = [column(part[4], 0) for part in parts]
        totals = [column(part[4], 64) for part in parts]
        top = functools.reduce(jnp.maximum, peaks)
        f = [jnp.exp2(p - top) for p in peaks]
        inverse = 1.0 / sum(a * b for a, b in zip(f, totals))
        for i in range(4):
            tile = sum(f[n] * parts[n][i] for n in range(4)) * inverse
            att[b, :, i * 128 : i * 128 + 128] = head_major(tile)

    def before(i):
        merge_core(i - 1)
        start_relay(i - 1)

    def services(i):
        if isinstance(i, int):
            if i >= TICK_R:
                relay(i - TICK_R)
            if i >= TICK_D:
                merge_first(i - TICK_D, True)
            return

        @pl.when(i >= TICK_R)
        def _():
            relay(i - TICK_R)

    def pair(j, _):
        for slot in range(2):
            i = 2 * j + slot
            attend(i, slot)
            copy_c(i).start()
            before(i)
            services(i)
        return 0

    scores(0, 0)
    attend(0, 0)
    pl.semaphore_wait(barrier, len(partners))
    copy_c(0).start()
    attend(1, 1)
    copy_c(1).start()
    before(1)
    lax.fori_loop(1, B // 2 - 1, pair, 0)
    attend(B - 2, 0)
    copy_c(B - 2).start()
    before(B - 2)
    services(B - 2)
    attend(B - 1, 1, False)
    copy_c(B - 1).start()
    merge_core(B - 2)
    send_p1(B - 2)
    services(B - 1)

    def late_relay(b, _):
        relay(b)
        return 0

    def late_relayed(b, _):
        merge_first(b, True)
        return 0

    def late_direct(b, _):
        merge_first(b, False)
        return 0

    def late_second(b, _):
        merge_second(b)
        return 0

    def second(start, stop):
        lax.fori_loop(start, stop, late_second, 0)

    merge_core(B - 1)
    send_p1(B - 1)
    lax.fori_loop(B - TICK_R, RELAYED, late_relay, 0)
    lax.fori_loop(B - TICK_D, 4, late_relayed, 0)
    second(0, 2)
    lax.fori_loop(4, RELAYED, late_relayed, 0)
    lax.fori_loop(RELAYED, B, late_direct, 0)

    sub = iota((8, 128), 0)

    def copy_y(n):
        ys, yr, _ = terms[3 * n : 3 * n + 3]
        return remote(ys.at[1 - c], yr, y_s.at[n], y_r.at[n], other)

    def copy_z(n, to):
        ys, _, zr = terms[3 * n : 3 * n + 3]
        chip = chip_at(CHIPS[to])
        return remote(ys.at[c, chip], zr.at[to], z_s.at[n, to], z_r.at[n, to], chip * 2 + c)

    def project(n):
        lo, hi = GROUPS[n]
        ys = terms[3 * n]
        low = att[lo:hi].reshape((hi - lo) * 8, L).astype(bf16)
        up = [jnp.dot(low, vu[h], preferred_element_type=f32) for h in range(2)]
        rows = []
        for b in range(0, hi - lo, 2):
            a = [up[h][8 * b : 8 * b + 8] for h in range(2)]
            z = [up[h][8 * b + 8 : 8 * b + 16] for h in range(2)]
            h0 = jnp.where(sub < 4, a[0], pltpu.roll(z[0], 4, 0))
            h1 = jnp.where(sub < 4, pltpu.roll(a[1], 4, 0), z[1])
            rows.append(jnp.concatenate([h0, h1], axis=1))
        head_out = jnp.concatenate(rows, axis=0).astype(bf16)
        for four in range(8):
            out = jnp.dot(head_out, w[:, four * 896 : four * 896 + 896], preferred_element_type=f32)
            for dev in range(4):
                start = dev * DEV_COLS
                low_tile = start // 128 * 128
                wide = out[:, low_tile : min(low_tile + 384, 896)]
                width = wide.shape[1]
                if start != low_tile:
                    wide = pltpu.roll(wide, width - (start - low_tile), 1)
                for rt in range(len(rows)):
                    for i in range(2):
                        ys[dev % 2, four * 2 + dev // 2, rt * 2 + i] = wide[
                            rt * 8 : rt * 8 + 8, i * 128 : i * 128 + 128
                        ]
        copy_y(n).start()

    def spread(n):
        ys, yr, _ = terms[3 * n : 3 * n + 3]
        copy_y(n).wait_recv()
        for chip in range(16):
            ys[c, chip] = ys[c, chip] + yr[chip]
        for to in range(15):
            copy_z(n, to).start()

    def finish(n):
        lo, hi = GROUPS[n]
        ys, _, zr = terms[3 * n : 3 * n + 3]
        for to in range(15):
            copy_z(n, to).wait_recv()
        done = ys[c, chip_at((0, 0))]
        for to in range(15):
            done = done + zr[to]
        for rt in range((hi - lo) // 2):
            tile = jnp.concatenate([done[rt * 2], done[rt * 2 + 1]], axis=1)[:, :DEV_COLS]
            for half in range(2):
                o_ref[lo + rt * 2 + half] = tile[half * 4 : half * 4 + 4]

    load_vu.wait()
    load_w.wait()
    second(2, GROUPS[0][1])
    project(0)
    second(GROUPS[0][1], B - 2)
    spread(0)
    second(B - 2, B)
    project(1)
    spread(1)
    finish(0)
    finish(1)

    def drain(b, _):
        copy_c(b).wait_send()

        @pl.when(b < RELAYED)
        def _():
            for way in range(2):
                copy_r(b, way).wait_send()

        @pl.when(b >= RELAYED)
        def _():
            copy_p1(b, 2).wait_send()

        for r in (1, 3):
            copy_p1(b, r).wait_send()
        for r in (1, 2, 3):
            copy_p2(b, r).wait_send()
        return 0

    lax.fori_loop(0, B, drain, 0)
    for n in range(len(GROUPS)):
        copy_y(n).wait_send()
        for to in range(15):
            copy_z(n, to).wait_send()


def local(queries, latent_cache, context_lengths, value_up, output_projection_rows):
    tile = (8, 128)
    dma = pltpu.SemaphoreType.DMA
    out = pl.pallas_call(
        kernel,
        out_shape=pltpu.VMEM((B, NQ, DEV_COLS), f32),
        in_specs=[
            pl.BlockSpec(memory_space=pl.ANY),
            pl.BlockSpec(memory_space=pl.ANY),
            pl.BlockSpec(memory_space=pltpu.SMEM),
            pl.BlockSpec(memory_space=pl.ANY),
            pl.BlockSpec(memory_space=pl.ANY),
        ],
        out_specs=pl.BlockSpec(memory_space=pltpu.VMEM),
        scratch_shapes=[
            pltpu.VMEM((B, ROWS, C), bf16),
            pltpu.VMEM((B, C, T), bf16),
            pltpu.VMEM((2, L, V), bf16),
            pltpu.VMEM((2 * V, D), bf16),
            pltpu.VMEM((2, ROWS, T), f32),
            pltpu.VMEM((2, ROWS, 128), f32),
            pltpu.VMEM((B, 2, 4, 17) + tile, f32),
            pltpu.VMEM((B, 4, 17) + tile, f32),
            pltpu.VMEM((B, 4, 17) + tile, f32),
            pltpu.VMEM((B, 2, 9) + tile, f32),
            pltpu.VMEM((B, 3, 17) + tile, f32),
            pltpu.VMEM((B, 4, 5) + tile, f32),
            pltpu.VMEM((B, 3, 5) + tile, f32),
            pltpu.VMEM((B, 8, L), f32),
            dma((3, B)),
            dma((B,)), dma((B,)),
            dma((B, 2)), dma((B, 2)),
            dma((B, 3)), dma((B, 3)),
            dma((B, 3)), dma((B, 3)),
            dma((len(GROUPS),)), dma((len(GROUPS),)),
            dma((len(GROUPS), 15)), dma((len(GROUPS), 15)),
        ]
        + [
            pltpu.VMEM(lead + (hi - lo,) + tile, f32)
            for lo, hi in GROUPS
            for lead in ((2, 16), (16,), (15,))
        ],
        compiler_params=pltpu.CompilerParams(
            collective_id=0, has_side_effects=True, vmem_limit_bytes=56 * 2**20
        ),
        name="attend_and_project",
    )(
        queries.reshape(B, ROWS, C),
        jnp.swapaxes(latent_cache, 1, 2),
        context_lengths,
        value_up,
        output_projection_rows,
    )
    return out.astype(bf16)


def solution(mesh):
    placed = (
        P("grp", None, None, None),
        P("grp", "seq", None),
        P("grp"),
        P("seq", None, None),
        P("seq", None),
    )
    return jax.shard_map(
        local, mesh=mesh, in_specs=placed, out_specs=P("grp", None, "seq"), check_vma=False
    )
```

```python
import functools

import jax
import jax.numpy as jnp
from jax import lax
from jax.experimental import pallas as pl
from jax.experimental.pallas import tpu as pltpu
from jax.sharding import PartitionSpec as P

MESH = pl.DeviceIdType.MESH
f32, bf16 = jnp.float32, jnp.bfloat16

B, NQ, H, T, C, L, V, D = 8, 4, 64, 1024, 576, 512, 128, 7168
ROWS = NQ * H
DEV_COLS = D // 32
C2 = 0.07216878364870323 * 1.4426950408889634
EMPTY = -1e30
TICK_R, TICK_D = 3, 6
RELAYED = 4
GROUPS = ((0, 4), (4, 8))
CHIPS = sorted(
    [(dx, dy) for dy in range(4) for dx in range(4) if dx or dy],
    key=lambda o: -(min(o[0], 4 - o[0]) + min(o[1], 4 - o[1])),
)


def iota(shape, dim):
    return lax.broadcasted_iota(jnp.int32, shape, dim)


def column(tile, lane):
    return jnp.broadcast_to(tile[:, lane : lane + 1], (8, 128))


def blocks_transposed(tiles):
    sub = iota((8, 128), 0)
    low, even = sub < 4, (sub & 2) == 0
    half = [pltpu.roll(t, 4, 0) for t in tiles]
    a0, a2 = jnp.where(low, tiles[0], half[2]), jnp.where(low, half[0], tiles[2])
    a1, a3 = jnp.where(low, tiles[1], half[3]), jnp.where(low, half[1], tiles[3])
    out = []
    for p, r in ((a0, a1), (a2, a3)):
        out.append(jnp.where(even, p, pltpu.roll(r, 2, 0)))
        out.append(jnp.where(even, pltpu.roll(p, 6, 0), r))
    return out


def tile_at(second, part):
    return second * 4 + part + second // 2


def head_major(tile):
    sub = iota((8, 128), 0)
    out = tile
    for to, at in ((1, 2), (2, 4), (3, 6), (4, 1), (5, 3), (6, 5)):
        out = jnp.where(sub == to, pltpu.roll(tile, (to - at) % 8, 0), out)
    return out


def kernel(
    q_hbm, k_hbm, ctx_ref, vu_hbm, w_hbm, o_ref,
    q, k, vu, w, sc, pk,
    pc, cr, mg, rr, p1r, p2, p2r, att,
    lsem, cs_s, cs_r, r_s, r_r, p1_s, p1_r, p2_s, p2_r, y_s, y_r, z_s, z_r, *terms
):
    me = lax.axis_index("seq")
    c, x, y = me % 2, (me // 2) % 4, me // 8

    def device(yy, xx, cc):
        return (yy * 4 + xx) * 2 + cc

    other = device(y, x, 1 - c)

    def along(par, r):
        return device((y + r * par) % 4, (x + r * (1 - par)) % 4, c)

    def position(par):
        return x + (y - x) * par

    barrier = pltpu.get_barrier_semaphore()
    def chip_at(offset):
        return ((y + offset[1]) % 4) * 4 + (x + offset[0]) % 4

    partners = [other] + [along(par, r) for par in (0, 1) for r in (1, 2, 3)]
    for to in partners:
        pl.semaphore_signal(barrier, inc=1, device_id={"seq": to}, device_id_type=MESH)

    def load_q(b):
        return pltpu.make_async_copy(q_hbm.at[b], q.at[b], lsem.at[0, b])

    def load_k(b):
        return pltpu.make_async_copy(k_hbm.at[b], k.at[b], lsem.at[1, b])

    load_vu = pltpu.make_async_copy(vu_hbm, vu, lsem.at[2, 0])
    load_w = pltpu.make_async_copy(w_hbm, w, lsem.at[2, 1])
    for b in range(B):
        load_q(b).start()
        load_k(b).start()
    load_vu.start()
    load_w.start()

    lane = iota((8, 128), 1)

    def remote(src, dst, ssem, rsem, to):
        return pltpu.make_async_remote_copy(
            src_ref=src, dst_ref=dst, send_sem=ssem, recv_sem=rsem,
            device_id={"seq": to}, device_id_type=MESH,
        )

    def copy_c(b):
        return remote(pc.at[b, 1 - c], cr.at[b], cs_s.at[b], cs_r.at[b], other)

    def copy_p1(b, r):
        return remote(
            mg.at[b, (position(b % 2) + r) % 4], p1r.at[b, r - 1],
            p1_s.at[b, r - 1], p1_r.at[b, r - 1], along(b % 2, r),
        )

    def copy_p2(b, r):
        return remote(
            p2.at[b, (position(1 - b % 2) + r) % 4], p2r.at[b, r - 1],
            p2_s.at[b, r - 1], p2_r.at[b, r - 1], along(1 - b % 2, r),
        )

    def scores(b, slot):
        load_q(b).wait()
        load_k(b).wait()
        s = jnp.dot(q[b], k[b], preferred_element_type=f32)
        limit = (ctx_ref[b] - (NQ - 1) - me * T) + (iota((ROWS, 1), 0) >> 6)
        s = jnp.where(iota((ROWS, T), 1) < limit, s, EMPTY)
        sc[slot] = s
        pk[slot] = jnp.broadcast_to(jnp.max(s, axis=1, keepdims=True), (ROWS, 128))

    def attend(b, slot, following=True):
        if following:
            scores(b + 1, 1 - slot)
        peak = pk[slot]
        e = jnp.exp2((sc[slot] - peak[:, :1]) * C2)
        total = jnp.sum(e, axis=1, keepdims=True)
        acc = lax.dot_general(
            e.astype(bf16), k[b, :L, :], (((1,), (1,)), ((), ())), preferred_element_type=f32
        )
        both = jnp.where(iota((ROWS, 128), 1) < 64, peak * C2, total)
        stats = {}
        for eight in range(8):
            rows = [slice(n * 64 + eight * 8, n * 64 + eight * 8 + 8) for n in range(4)]
            for part in range(5):
                src = both if part == 4 else acc[:, part * 128 : part * 128 + 128]
                for n, tile in enumerate(blocks_transposed([src[r] for r in rows])):
                    chip, core = (eight * 4 + n) // 2, n % 2
                    yy, xx = chip // 4, chip % 4
                    first, second = (xx, yy) if slot == 0 else (yy, xx)
                    if part < 4:
                        pc[b, core, first, tile_at(second, part)] = tile
                    else:
                        before = stats.get((core, first), jnp.zeros((8, 128), f32))
                        stats[core, first] = jnp.where((lane & 63) == second, tile, before)
        for (core, first), tile in stats.items():
            pc[b, core, first, 8] = tile

    def merge_stats(stats):
        top = functools.reduce(jnp.maximum, stats)
        shares = [jnp.exp2(s - top) for s in stats]
        total = sum(pltpu.roll(f, 64, 1) * s for f, s in zip(shares, stats))
        return shares, jnp.where(lane < 64, top, total)

    def merge_core(b):
        copy_c(b).wait_recv()
        merged = [merge_stats([pc[b, c, g, 8], cr[b, g, 8]]) for g in range(4)]
        factors = [[[column(s, t) for s in shares] for t in range(4)] for shares, _ in merged]
        for g in range(4):
            own, got = pc[b, c, g], cr[b, g]
            sums = {8: merged[g][1]}
            for t in range(4):
                f0, f1 = factors[g][t]
                for i in range(4):
                    at = tile_at(t, i)
                    sums[at] = f0 * own[at] + f1 * got[at]
            for at, tile in sums.items():
                mg[b, g, at] = tile

    def copy_r(b, way):
        par = b % 2
        return remote(
            mg.at[b, (position(par) + 2) % 4, pl.ds(8 * way, 9)], rr.at[b, way],
            r_s.at[b, way], r_r.at[b, way], along(par, 1 + 2 * way),
        )

    def start_relay(b):
        for way in range(2):
            copy_r(b, way).start()

    def relay(b):
        for way in range(2):
            copy_r(b, way).wait_recv()
        sums = []
        for way in range(2):
            g = (position(b % 2) + 1 + 2 * way) % 4
            own, got = mg[b, g, pl.ds(8 * way, 9)], rr[b, way]
            stat_at = 8 - 8 * way
            shares, stat = merge_stats([own[stat_at], got[stat_at]])
            sums.append((g, 8, jnp.where((lane & 63) // 2 == way, stat, own[stat_at])))
            for t in (2 * way, 2 * way + 1):
                f0, f1 = column(shares[0], t), column(shares[1], t)
                for i in range(4):
                    at = tile_at(t, i)
                    sums.append((g, at, f0 * own[at - 8 * way] + f1 * got[at - 8 * way]))
        for g, at, tile in sums:
            mg[b, g, at] = tile
        for way in range(2):
            copy_p1(b, 1 + 2 * way).start()

    def send_p1(b):
        for r in (2, 1, 3):
            copy_p1(b, r).start()

    def merge_first(b, relayed):
        steps = (1, 3) if relayed else (1, 2, 3)
        for r in steps:
            copy_p1(b, r).wait_recv()
        parts = [mg.at[b, position(b % 2)]] + [p1r.at[b, r - 1] for r in steps]
        shares, stat = merge_stats([part[8] for part in parts])
        factors = [[column(s, t) for s in shares] for t in range(4)]
        sums = []
        for t in range(4):
            f = factors[t]
            sums += [
                (t, i, sum(f[n] * parts[n][tile_at(t, i)] for n in range(len(parts))))
                for i in range(4)
            ]
            sums.append((t, 4, pltpu.roll(stat, 128 - t, 1) if t else stat))
        for t, i, tile in sums:
            p2[b, t, i] = tile
        for r in (2, 1, 3):
            copy_p2(b, r).start()

    def merge_second(b):
        for r in (1, 2, 3):
            copy_p2(b, r).wait_recv()
        parts = [p2.at[b, position(1 - b % 2)]] + [p2r.at[b, r] for r in range(3)]
        peaks = [column(part[4], 0) for part in parts]
        totals = [column(part[4], 64) for part in parts]
        top = functools.reduce(jnp.maximum, peaks)
        f = [jnp.exp2(p - top) for p in peaks]
        inverse = 1.0 / sum(a * b for a, b in zip(f, totals))
        tiles = [head_major(sum(f[n] * parts[n][i] for n in range(4)) * inverse) for i in range(4)]
        for i, tile in enumerate(tiles):
            att[b, :, i * 128 : i * 128 + 128] = tile

    def before(i):
        merge_core(i - 1)
        if isinstance(i, int):
            (start_relay if i - 1 < RELAYED else send_p1)(i - 1)
        elif RELAYED >= B - 3:
            start_relay(i - 1)
        else:
            pl.when(i - 1 < RELAYED)(lambda: start_relay(i - 1))
            pl.when(i - 1 >= RELAYED)(lambda: send_p1(i - 1))

    def services(i):
        if isinstance(i, int):
            if TICK_R <= i < TICK_R + RELAYED:
                relay(i - TICK_R)
            if i >= TICK_D:
                merge_first(i - TICK_D, True)
            return

        @pl.when(i >= TICK_R)
        def _():
            relay(i - TICK_R)

    def pair(j, _):
        for slot in range(2):
            i = 2 * j + slot
            attend(i, slot)
            copy_c(i).start()
            before(i)
            services(i)
        return 0

    scores(0, 0)
    attend(0, 0)
    pl.semaphore_wait(barrier, len(partners))
    copy_c(0).start()
    attend(1, 1)
    copy_c(1).start()
    before(1)
    lax.fori_loop(1, B // 2 - 1, pair, 0)
    attend(B - 2, 0)
    copy_c(B - 2).start()
    before(B - 2)
    services(B - 2)
    attend(B - 1, 1, False)
    copy_c(B - 1).start()
    before(B - 1)
    services(B - 1)

    def late_relayed(b, _):
        merge_first(b, True)
        return 0

    def late_direct(b, _):
        merge_first(b, False)
        return 0

    def late_second(b, _):
        merge_second(b)
        return 0

    def second(start, stop):
        lax.fori_loop(start, stop, late_second, 0)

    merge_core(B - 1)
    send_p1(B - 1)
    for b in range(B - TICK_R, RELAYED):
        relay(b)
    lax.fori_loop(B - TICK_D, 4, late_relayed, 0)
    second(0, 2)
    if RELAYED > 4:
        lax.fori_loop(4, RELAYED, late_relayed, 0)
    lax.fori_loop(RELAYED, B, late_direct, 0)

    sub = iota((8, 128), 0)

    def copy_y(n):
        ys, yr, _ = terms[3 * n : 3 * n + 3]
        return remote(ys.at[1 - c], yr, y_s.at[n], y_r.at[n], other)

    def copy_z(n, to):
        ys, _, zr = terms[3 * n : 3 * n + 3]
        chip = chip_at(CHIPS[to])
        return remote(ys.at[c, chip], zr.at[to], z_s.at[n, to], z_r.at[n, to], chip * 2 + c)

    def project(n):
        lo, hi = GROUPS[n]
        ys = terms[3 * n]
        low = att[lo:hi].reshape((hi - lo) * 8, L).astype(bf16)
        up = [jnp.dot(low, vu[h], preferred_element_type=f32) for h in range(2)]
        rows = []
        for b in range(0, hi - lo, 2):
            a = [up[h][8 * b : 8 * b + 8] for h in range(2)]
            z = [up[h][8 * b + 8 : 8 * b + 16] for h in range(2)]
            h0 = jnp.where(sub < 4, a[0], pltpu.roll(z[0], 4, 0))
            h1 = jnp.where(sub < 4, pltpu.roll(a[1], 4, 0), z[1])
            rows.append(jnp.concatenate([h0, h1], axis=1))
        head_out = jnp.concatenate(rows, axis=0).astype(bf16)
        for four in range(8):
            out = jnp.dot(head_out, w[:, four * 896 : four * 896 + 896], preferred_element_type=f32)
            for dev in range(4):
                start = dev * DEV_COLS
                low_tile = start // 128 * 128
                wide = out[:, low_tile : min(low_tile + 384, 896)]
                width = wide.shape[1]
                if start != low_tile:
                    wide = pltpu.roll(wide, width - (start - low_tile), 1)
                for rt in range(len(rows)):
                    for i in range(2):
                        ys[dev % 2, four * 2 + dev // 2, rt * 2 + i] = wide[
                            rt * 8 : rt * 8 + 8, i * 128 : i * 128 + 128
                        ]
        copy_y(n).start()

    def spread(n):
        ys, yr, _ = terms[3 * n : 3 * n + 3]
        copy_y(n).wait_recv()
        for chip in range(16):
            ys[c, chip] = ys[c, chip] + yr[chip]
        for to in range(15):
            copy_z(n, to).start()

    def finish(n):
        lo, hi = GROUPS[n]
        ys, _, zr = terms[3 * n : 3 * n + 3]
        for to in range(15):
            copy_z(n, to).wait_recv()
        done = ys[c, chip_at((0, 0))]
        for to in range(15):
            done = done + zr[to]
        for rt in range((hi - lo) // 2):
            tile = jnp.concatenate([done[rt * 2], done[rt * 2 + 1]], axis=1)[:, :DEV_COLS]
            for half in range(2):
                o_ref[lo + rt * 2 + half] = tile[half * 4 : half * 4 + 4]

    load_vu.wait()
    load_w.wait()
    at = 2
    for n, (_, hi) in enumerate(GROUPS[:-1]):
        second(at, hi)
        project(n)
        at = hi
    second(at, B - 2)
    spread(0)
    second(max(at, B - 2), B)
    project(len(GROUPS) - 1)
    for n in range(1, len(GROUPS)):
        spread(n)

    def drain(b, _):
        copy_c(b).wait_send()

        @pl.when(b < RELAYED)
        def _():
            for way in range(2):
                copy_r(b, way).wait_send()

        @pl.when(b >= RELAYED)
        def _():
            copy_p1(b, 2).wait_send()

        for r in (1, 3):
            copy_p1(b, r).wait_send()
        for r in (1, 2, 3):
            copy_p2(b, r).wait_send()
        return 0

    lax.fori_loop(0, B, drain, 0)
    for n in range(len(GROUPS)):
        copy_y(n).wait_send()
        for to in range(15):
            copy_z(n, to).wait_send()
    for n in range(len(GROUPS)):
        finish(n)


def local(queries, latent_cache, context_lengths, value_up, output_projection_rows):
    tile = (8, 128)
    dma = pltpu.SemaphoreType.DMA
    out = pl.pallas_call(
        kernel,
        out_shape=pltpu.VMEM((B, NQ, DEV_COLS), f32),
        in_specs=[
            pl.BlockSpec(memory_space=pl.ANY),
            pl.BlockSpec(memory_space=pl.ANY),
            pl.BlockSpec(memory_space=pltpu.SMEM),
            pl.BlockSpec(memory_space=pl.ANY),
            pl.BlockSpec(memory_space=pl.ANY),
        ],
        out_specs=pl.BlockSpec(memory_space=pltpu.VMEM),
        scratch_shapes=[
            pltpu.VMEM((B, ROWS, C), bf16),
            pltpu.VMEM((B, C, T), bf16),
            pltpu.VMEM((2, L, V), bf16),
            pltpu.VMEM((2 * V, D), bf16),
            pltpu.VMEM((2, ROWS, T), f32),
            pltpu.VMEM((2, ROWS, 128), f32),
            pltpu.VMEM((B, 2, 4, 17) + tile, f32),
            pltpu.VMEM((B, 4, 17) + tile, f32),
            pltpu.VMEM((B, 4, 17) + tile, f32),
            pltpu.VMEM((B, 2, 9) + tile, f32),
            pltpu.VMEM((B, 3, 17) + tile, f32),
            pltpu.VMEM((B, 4, 5) + tile, f32),
            pltpu.VMEM((B, 3, 5) + tile, f32),
            pltpu.VMEM((B, 8, L), f32),
            dma((3, B)),
            dma((B,)), dma((B,)),
            dma((B, 2)), dma((B, 2)),
            dma((B, 3)), dma((B, 3)),
            dma((B, 3)), dma((B, 3)),
            dma((len(GROUPS),)), dma((len(GROUPS),)),
            dma((len(GROUPS), 15)), dma((len(GROUPS), 15)),
        ]
        + [
            pltpu.VMEM(lead + (hi - lo,) + tile, f32)
            for lo, hi in GROUPS
            for lead in ((2, 16), (16,), (15,))
        ],
        compiler_params=pltpu.CompilerParams(
            collective_id=0, has_side_effects=True, vmem_limit_bytes=56 * 2**20
        ),
        name="attend_and_project",
    )(
        queries.reshape(B, ROWS, C),
        jnp.swapaxes(latent_cache, 1, 2),
        context_lengths,
        value_up,
        output_projection_rows,
    )
    return out.astype(bf16)


def solution(mesh):
    placed = (
        P("grp", None, None, None),
        P("grp", "seq", None),
        P("grp"),
        P("seq", None, None),
        P("seq", None),
    )
    return jax.shard_map(
        local, mesh=mesh, in_specs=placed, out_specs=P("grp", None, "seq"), check_vma=False
    )
```

```python
import functools

import jax
import jax.numpy as jnp
from jax import lax
from jax.experimental import pallas as pl
from jax.experimental.pallas import tpu as pltpu
from jax.sharding import PartitionSpec as P

MESH = pl.DeviceIdType.MESH
f32, bf16 = jnp.float32, jnp.bfloat16

B, NQ, H, T, C, L, V, D = 8, 4, 64, 1024, 576, 512, 128, 7168
ROWS = NQ * H
DEV_COLS = D // 32
C2 = 0.07216878364870323 * 1.4426950408889634
EMPTY = -1e30
TICK_R, TICK_D = 3, 6
RELAYED = 4
GROUPS = ((0, 6), (6, 8))
CHIPS = sorted(
    [(dx, dy) for dy in range(4) for dx in range(4) if dx or dy],
    key=lambda o: -(min(o[0], 4 - o[0]) + min(o[1], 4 - o[1])),
)


def iota(shape, dim):
    return lax.broadcasted_iota(jnp.int32, shape, dim)


def column(tile, lane):
    return jnp.broadcast_to(tile[:, lane : lane + 1], (8, 128))


def blocks_transposed(tiles):
    sub = iota((8, 128), 0)
    low, even = sub < 4, (sub & 2) == 0
    half = [pltpu.roll(t, 4, 0) for t in tiles]
    a0, a2 = jnp.where(low, tiles[0], half[2]), jnp.where(low, half[0], tiles[2])
    a1, a3 = jnp.where(low, tiles[1], half[3]), jnp.where(low, half[1], tiles[3])
    out = []
    for p, r in ((a0, a1), (a2, a3)):
        out.append(jnp.where(even, p, pltpu.roll(r, 2, 0)))
        out.append(jnp.where(even, pltpu.roll(p, 6, 0), r))
    return out


def tile_at(second, part):
    return second * 4 + part + second // 2


def head_major(tile):
    sub = iota((8, 128), 0)
    out = tile
    for to, at in ((1, 2), (2, 4), (3, 6), (4, 1), (5, 3), (6, 5)):
        out = jnp.where(sub == to, pltpu.roll(tile, (to - at) % 8, 0), out)
    return out


def kernel(
    q_hbm, k_hbm, ctx_ref, vu_hbm, w_hbm, o_ref,
    q, k, vu, w, sc, pk,
    pc, cr, mg, rr, p1r, p2, p2r, att,
    lsem, cs_s, cs_r, r_s, r_r, p1_s, p1_r, p2_s, p2_r, y_s, y_r, z_s, z_r, *terms
):
    me = lax.axis_index("seq")
    c, x, y = me % 2, (me // 2) % 4, me // 8

    def device(yy, xx, cc):
        return (yy * 4 + xx) * 2 + cc

    other = device(y, x, 1 - c)

    def along(par, r):
        return device((y + r * par) % 4, (x + r * (1 - par)) % 4, c)

    def position(par):
        return x + (y - x) * par

    barrier = pltpu.get_barrier_semaphore()
    def chip_at(offset):
        return ((y + offset[1]) % 4) * 4 + (x + offset[0]) % 4

    partners = [other] + [along(par, r) for par in (0, 1) for r in (1, 2, 3)]
    for to in partners:
        pl.semaphore_signal(barrier, inc=1, device_id={"seq": to}, device_id_type=MESH)

    def load_q(b):
        return pltpu.make_async_copy(q_hbm.at[b], q.at[b], lsem.at[0, b])

    def load_k(b):
        return pltpu.make_async_copy(k_hbm.at[b], k.at[b], lsem.at[1, b])

    load_vu = pltpu.make_async_copy(vu_hbm, vu, lsem.at[2, 0])
    load_w = pltpu.make_async_copy(w_hbm, w, lsem.at[2, 1])
    for b in range(B):
        load_q(b).start()
        load_k(b).start()
    load_vu.start()
    load_w.start()

    lane = iota((8, 128), 1)

    def remote(src, dst, ssem, rsem, to):
        return pltpu.make_async_remote_copy(
            src_ref=src, dst_ref=dst, send_sem=ssem, recv_sem=rsem,
            device_id={"seq": to}, device_id_type=MESH,
        )

    def copy_c(b):
        return remote(pc.at[b, 1 - c], cr.at[b], cs_s.at[b], cs_r.at[b], other)

    def copy_p1(b, r):
        return remote(
            mg.at[b, (position(b % 2) + r) % 4], p1r.at[b, r - 1],
            p1_s.at[b, r - 1], p1_r.at[b, r - 1], along(b % 2, r),
        )

    def copy_p2(b, r):
        return remote(
            p2.at[b, (position(1 - b % 2) + r) % 4], p2r.at[b, r - 1],
            p2_s.at[b, r - 1], p2_r.at[b, r - 1], along(1 - b % 2, r),
        )

    def scores(b, slot):
        load_q(b).wait()
        load_k(b).wait()
        s = jnp.dot(q[b], k[b], preferred_element_type=f32)
        limit = (ctx_ref[b] - (NQ - 1) - me * T) + (iota((ROWS, 1), 0) >> 6)
        s = jnp.where(iota((ROWS, T), 1) < limit, s, EMPTY)
        sc[slot] = s
        pk[slot] = jnp.broadcast_to(jnp.max(s, axis=1, keepdims=True), (ROWS, 128))

    def attend(b, slot, following=True):
        if following:
            scores(b + 1, 1 - slot)
        peak = pk[slot]
        e = jnp.exp2((sc[slot] - peak[:, :1]) * C2)
        total = jnp.sum(e, axis=1, keepdims=True)
        acc = lax.dot_general(
            e.astype(bf16), k[b, :L, :], (((1,), (1,)), ((), ())), preferred_element_type=f32
        )
        both = jnp.where(iota((ROWS, 128), 1) < 64, peak * C2, total)
        stats = {}
        for eight in range(8):
            rows = [slice(n * 64 + eight * 8, n * 64 + eight * 8 + 8) for n in range(4)]
            for part in range(5):
                src = both if part == 4 else acc[:, part * 128 : part * 128 + 128]
                for n, tile in enumerate(blocks_transposed([src[r] for r in rows])):
                    chip, core = (eight * 4 + n) // 2, n % 2
                    yy, xx = chip // 4, chip % 4
                    first, second = (xx, yy) if slot == 0 else (yy, xx)
                    if part < 4:
                        pc[b, core, first, tile_at(second, part)] = tile
                    else:
                        before = stats.get((core, first), jnp.zeros((8, 128), f32))
                        stats[core, first] = jnp.where((lane & 63) == second, tile, before)
        for (core, first), tile in stats.items():
            pc[b, core, first, 8] = tile

    def merge_stats(stats):
        top = functools.reduce(jnp.maximum, stats)
        shares = [jnp.exp2(s - top) for s in stats]
        total = sum(pltpu.roll(f, 64, 1) * s for f, s in zip(shares, stats))
        return shares, jnp.where(lane < 64, top, total)

    def merge_core(b):
        copy_c(b).wait_recv()
        merged = [merge_stats([pc[b, c, g, 8], cr[b, g, 8]]) for g in range(4)]
        factors = [[[column(s, t) for s in shares] for t in range(4)] for shares, _ in merged]
        for g in range(4):
            own, got = pc[b, c, g], cr[b, g]
            sums = {8: merged[g][1]}
            for t in range(4):
                f0, f1 = factors[g][t]
                for i in range(4):
                    at = tile_at(t, i)
                    sums[at] = f0 * own[at] + f1 * got[at]
            for at, tile in sums.items():
                mg[b, g, at] = tile

    def copy_r(b, way):
        par = b % 2
        return remote(
            mg.at[b, (position(par) + 2) % 4, pl.ds(8 * way, 9)], rr.at[b, way],
            r_s.at[b, way], r_r.at[b, way], along(par, 1 + 2 * way),
        )

    def start_relay(b):
        for way in range(2):
            copy_r(b, way).start()

    def relay(b):
        for way in range(2):
            copy_r(b, way).wait_recv()
        sums = []
        for way in range(2):
            g = (position(b % 2) + 1 + 2 * way) % 4
            own, got = mg[b, g, pl.ds(8 * way, 9)], rr[b, way]
            stat_at = 8 - 8 * way
            shares, stat = merge_stats([own[stat_at], got[stat_at]])
            sums.append((g, 8, jnp.where((lane & 63) // 2 == way, stat, own[stat_at])))
            for t in (2 * way, 2 * way + 1):
                f0, f1 = column(shares[0], t), column(shares[1], t)
                for i in range(4):
                    at = tile_at(t, i)
                    sums.append((g, at, f0 * own[at - 8 * way] + f1 * got[at - 8 * way]))
        for g, at, tile in sums:
            mg[b, g, at] = tile
        for way in range(2):
            copy_p1(b, 1 + 2 * way).start()

    def send_p1(b):
        for r in (2, 1, 3):
            copy_p1(b, r).start()

    def merge_first(b, relayed):
        steps = (1, 3) if relayed else (1, 2, 3)
        for r in steps:
            copy_p1(b, r).wait_recv()
        parts = [mg.at[b, position(b % 2)]] + [p1r.at[b, r - 1] for r in steps]
        shares, stat = merge_stats([part[8] for part in parts])
        factors = [[column(s, t) for s in shares] for t in range(4)]
        sums = []
        for t in range(4):
            f = factors[t]
            sums += [
                (t, i, sum(f[n] * parts[n][tile_at(t, i)] for n in range(len(parts))))
                for i in range(4)
            ]
            sums.append((t, 4, pltpu.roll(stat, 128 - t, 1) if t else stat))
        for t, i, tile in sums:
            p2[b, t, i] = tile
        for r in (2, 1, 3):
            copy_p2(b, r).start()

    def merge_second(b):
        for r in (1, 2, 3):
            copy_p2(b, r).wait_recv()
        parts = [p2.at[b, position(1 - b % 2)]] + [p2r.at[b, r] for r in range(3)]
        peaks = [column(part[4], 0) for part in parts]
        totals = [column(part[4], 64) for part in parts]
        top = functools.reduce(jnp.maximum, peaks)
        f = [jnp.exp2(p - top) for p in peaks]
        inverse = 1.0 / sum(a * b for a, b in zip(f, totals))
        tiles = [head_major(sum(f[n] * parts[n][i] for n in range(4)) * inverse) for i in range(4)]
        for i, tile in enumerate(tiles):
            att[b, :, i * 128 : i * 128 + 128] = tile

    def before(i):
        merge_core(i - 1)
        if isinstance(i, int):
            (start_relay if i - 1 < RELAYED else send_p1)(i - 1)
        elif RELAYED >= B - 3:
            start_relay(i - 1)
        else:
            pl.when(i - 1 < RELAYED)(lambda: start_relay(i - 1))
            pl.when(i - 1 >= RELAYED)(lambda: send_p1(i - 1))

    def services(i):
        if isinstance(i, int):
            if TICK_R <= i < TICK_R + RELAYED:
                relay(i - TICK_R)
            if i >= TICK_D:
                merge_first(i - TICK_D, True)
            return

        @pl.when(i >= TICK_R)
        def _():
            relay(i - TICK_R)

    def pair(j, _):
        for slot in range(2):
            i = 2 * j + slot
            attend(i, slot)
            copy_c(i).start()
            before(i)
            services(i)
        return 0

    scores(0, 0)
    attend(0, 0)
    pl.semaphore_wait(barrier, len(partners))
    copy_c(0).start()
    attend(1, 1)
    copy_c(1).start()
    before(1)
    lax.fori_loop(1, B // 2 - 1, pair, 0)
    attend(B - 2, 0)
    copy_c(B - 2).start()
    before(B - 2)
    services(B - 2)
    attend(B - 1, 1, False)
    copy_c(B - 1).start()
    before(B - 1)
    services(B - 1)

    def late_relayed(b, _):
        merge_first(b, True)
        return 0

    def late_direct(b, _):
        merge_first(b, False)
        return 0

    def late_second(b, _):
        merge_second(b)
        return 0

    def second(start, stop):
        lax.fori_loop(start, stop, late_second, 0)

    merge_core(B - 1)
    send_p1(B - 1)
    for b in range(B - TICK_R, RELAYED):
        relay(b)
    lax.fori_loop(B - TICK_D, 4, late_relayed, 0)
    second(0, 2)
    if RELAYED > 4:
        lax.fori_loop(4, RELAYED, late_relayed, 0)
    lax.fori_loop(RELAYED, B, late_direct, 0)

    sub = iota((8, 128), 0)

    def copy_y(n):
        ys, yr, _ = terms[3 * n : 3 * n + 3]
        return remote(ys.at[1 - c], yr, y_s.at[n], y_r.at[n], other)

    def copy_z(n, to):
        ys, _, zr = terms[3 * n : 3 * n + 3]
        chip = chip_at(CHIPS[to])
        return remote(ys.at[c, chip], zr.at[to], z_s.at[n, to], z_r.at[n, to], chip * 2 + c)

    def project(n):
        lo, hi = GROUPS[n]
        ys = terms[3 * n]
        low = att[lo:hi].reshape((hi - lo) * 8, L).astype(bf16)
        up = [jnp.dot(low, vu[h], preferred_element_type=f32) for h in range(2)]
        rows = []
        for b in range(0, hi - lo, 2):
            a = [up[h][8 * b : 8 * b + 8] for h in range(2)]
            z = [up[h][8 * b + 8 : 8 * b + 16] for h in range(2)]
            h0 = jnp.where(sub < 4, a[0], pltpu.roll(z[0], 4, 0))
            h1 = jnp.where(sub < 4, pltpu.roll(a[1], 4, 0), z[1])
            rows.append(jnp.concatenate([h0, h1], axis=1))
        head_out = jnp.concatenate(rows, axis=0).astype(bf16)
        for four in range(8):
            out = jnp.dot(head_out, w[:, four * 896 : four * 896 + 896], preferred_element_type=f32)
            for dev in range(4):
                start = dev * DEV_COLS
                low_tile = start // 128 * 128
                wide = out[:, low_tile : min(low_tile + 384, 896)]
                width = wide.shape[1]
                if start != low_tile:
                    wide = pltpu.roll(wide, width - (start - low_tile), 1)
                for rt in range(len(rows)):
                    for i in range(2):
                        ys[dev % 2, four * 2 + dev // 2, rt * 2 + i] = wide[
                            rt * 8 : rt * 8 + 8, i * 128 : i * 128 + 128
                        ]
        copy_y(n).start()

    def spread(n):
        ys, yr, _ = terms[3 * n : 3 * n + 3]
        copy_y(n).wait_recv()
        for chip in range(16):
            ys[c, chip] = ys[c, chip] + yr[chip]
        for to in range(15):
            copy_z(n, to).start()

    def finish(n):
        lo, hi = GROUPS[n]
        ys, _, zr = terms[3 * n : 3 * n + 3]
        for to in range(15):
            copy_z(n, to).wait_recv()
        done = ys[c, chip_at((0, 0))]
        for to in range(15):
            done = done + zr[to]
        for rt in range((hi - lo) // 2):
            tile = jnp.concatenate([done[rt * 2], done[rt * 2 + 1]], axis=1)[:, :DEV_COLS]
            for half in range(2):
                o_ref[lo + rt * 2 + half] = tile[half * 4 : half * 4 + 4]

    load_vu.wait()
    load_w.wait()
    at = 2
    for n, (_, hi) in enumerate(GROUPS[:-1]):
        second(at, hi)
        project(n)
        at = hi
    second(at, B - 2)
    spread(0)
    second(max(at, B - 2), B)
    project(len(GROUPS) - 1)
    for n in range(1, len(GROUPS)):
        spread(n)

    def drain(b, _):
        copy_c(b).wait_send()

        @pl.when(b < RELAYED)
        def _():
            for way in range(2):
                copy_r(b, way).wait_send()

        @pl.when(b >= RELAYED)
        def _():
            copy_p1(b, 2).wait_send()

        for r in (1, 3):
            copy_p1(b, r).wait_send()
        for r in (1, 2, 3):
            copy_p2(b, r).wait_send()
        return 0

    lax.fori_loop(0, B, drain, 0)
    for n in range(len(GROUPS)):
        copy_y(n).wait_send()
        for to in range(15):
            copy_z(n, to).wait_send()
    for n in range(len(GROUPS)):
        finish(n)


def local(queries, latent_cache, context_lengths, value_up, output_projection_rows):
    tile = (8, 128)
    dma = pltpu.SemaphoreType.DMA
    out = pl.pallas_call(
        kernel,
        out_shape=pltpu.VMEM((B, NQ, DEV_COLS), f32),
        in_specs=[
            pl.BlockSpec(memory_space=pl.ANY),
            pl.BlockSpec(memory_space=pl.ANY),
            pl.BlockSpec(memory_space=pltpu.SMEM),
            pl.BlockSpec(memory_space=pl.ANY),
            pl.BlockSpec(memory_space=pl.ANY),
        ],
        out_specs=pl.BlockSpec(memory_space=pltpu.VMEM),
        scratch_shapes=[
            pltpu.VMEM((B, ROWS, C), bf16),
            pltpu.VMEM((B, C, T), bf16),
            pltpu.VMEM((2, L, V), bf16),
            pltpu.VMEM((2 * V, D), bf16),
            pltpu.VMEM((2, ROWS, T), f32),
            pltpu.VMEM((2, ROWS, 128), f32),
            pltpu.VMEM((B, 2, 4, 17) + tile, f32),
            pltpu.VMEM((B, 4, 17) + tile, f32),
            pltpu.VMEM((B, 4, 17) + tile, f32),
            pltpu.VMEM((B, 2, 9) + tile, f32),
            pltpu.VMEM((B, 3, 17) + tile, f32),
            pltpu.VMEM((B, 4, 5) + tile, f32),
            pltpu.VMEM((B, 3, 5) + tile, f32),
            pltpu.VMEM((B, 8, L), f32),
            dma((3, B)),
            dma((B,)), dma((B,)),
            dma((B, 2)), dma((B, 2)),
            dma((B, 3)), dma((B, 3)),
            dma((B, 3)), dma((B, 3)),
            dma((len(GROUPS),)), dma((len(GROUPS),)),
            dma((len(GROUPS), 15)), dma((len(GROUPS), 15)),
        ]
        + [
            pltpu.VMEM(lead + (hi - lo,) + tile, f32)
            for lo, hi in GROUPS
            for lead in ((2, 16), (16,), (15,))
        ],
        compiler_params=pltpu.CompilerParams(
            collective_id=0, has_side_effects=True, vmem_limit_bytes=56 * 2**20
        ),
        name="attend_and_project",
    )(
        queries.reshape(B, ROWS, C),
        jnp.swapaxes(latent_cache, 1, 2),
        context_lengths,
        value_up,
        output_projection_rows,
    )
    return out.astype(bf16)


def solution(mesh):
    placed = (
        P("grp", None, None, None),
        P("grp", "seq", None),
        P("grp"),
        P("seq", None, None),
        P("seq", None),
    )
    return jax.shard_map(
        local, mesh=mesh, in_specs=placed, out_specs=P("grp", None, "seq"), check_vma=False
    )
```
